32 devices in a mesh: replica: 2 (over x), fsdp: 16 (over z, y, core).
Axes of the slice: x: 2, y: 2, z: 4, core: 2. Of those that a mesh axis runs over, the one named last changes fastest.
Arguments:
- tokens: bfloat16 [8192, 7168], P(('replica', 'fsdp')), may hold values from -6 to 6
- cotangent: bfloat16 [8192, 128], P(('replica', 'fsdp')), may hold values from -0.09375 to 0.09375
- keep_mask: int32 [8192], P(('replica', 'fsdp')), may hold values 0 or 1
- key_weight: bfloat16 [2, 7168, 128], P('replica', 'fsdp'), may hold values from -0.0625 to 0.0625
- norm_gain: float32 [2, 7168], P('replica', 'fsdp'), may hold values from 0.1 to 1.9
- local_params: float32 [2, 8, 65536], P('replica', None, 'fsdp'), may hold values from -1400 to 1400
- global_params: float32 [8, 65536], P(None, 'fsdp'), may hold values from -4 to 4
- momentum: float32 [8, 65536], P(None, 'fsdp'), may hold values from -6 to 6
- fragment_order: int32 [8], replicated, may hold values from 0 to 7, each once
Outputs:
- weight_grad: float32 [2, 7168, 128], P('replica', 'fsdp')
- gain_grad: float32 [2, 7168], P('replica', 'fsdp')
- local_out: float32 [2, 8, 65536], P('replica', None, 'fsdp')
- global_out: float32 [8, 65536], P(None, 'fsdp')
- moment_out: float32 [8, 65536], P(None, 'fsdp')
The draws below stay inside these ranges and needn't reach their ends.
Inputs may be any that keep to these rules, and one draw needn't show every extreme that they name: `fragment_order`: its first 2 entries name the fragment's layers.
All inputs are finite; a program needn't handle non-finite values. No bound on the sum of `keep_mask` on one device may be relied on, other than what follows from the above.
Results may differ from the reference program's by a relative error of at most 0.005.
Values may be sent and summed in bfloat16 or wider, within the bound.
No kernel may reach another device: no remote copies, remote signals or barrier semaphores. Data moves between devices by JAX's collectives and lax.ppermute only.
A program may use at most 64 MiB of HBM per device.

```python
import jax
import jax.numpy as jnp
from jax import lax

D = 7168
HD = 128
TOK_DEV = 256
P_DEV = 4096
HELD = 8
FRAG = 2
REPLICAS = 2
TOKENS = 8192
P_ALL = 65536
N_FSDP = 16


def common_base(key):
    return jax.random.truncated_normal(key, -4.0, 4.0, (HELD, P_ALL), jnp.float32)


def draw_global_params(key, part):
    base = common_base(key)
    return base


def draw_local_params(key, part):
    base = common_base(key)
    key = jax.random.fold_in(key, 2)
    key_row, key_col, key_own = jax.random.split(key, 3)
    row_scale = jnp.exp(jax.random.uniform(key_row, (1, HELD, 1), jnp.float32) * 2.302585)
    col_scale = jnp.exp(jax.random.uniform(key_col, (1, 1, P_ALL), jnp.float32) * 2.302585)
    shard = (jnp.arange(P_ALL) // P_DEV).astype(jnp.float32)
    ramp = 1.0 + 2.0 * shard / max(P_ALL // P_DEV - 1, 1)
    noise = jax.random.truncated_normal(key_own, -4.0, 4.0, (REPLICAS, HELD, P_ALL), jnp.float32)
    return base[None] + 0.3 * row_scale * col_scale * ramp[None, None, :] * noise


def place_ends(values, own_key, low, high):
    longest = values.shape.index(max(values.shape))
    spots = []
    for shift in (0, 1):
        where = [jax.random.randint(jax.random.fold_in(own_key, axis), (), 0, length) for axis, length in enumerate(values.shape)]
        where[longest] = (where[longest] + shift) % values.shape[longest]
        spots.append(tuple(where))
    return values.at[spots[0]].set(low).at[spots[1]].set(high)


def strengthened(drawn, stream_key, source, target, blocks, factor):
    def block_of(position):
        return (jnp.arange(drawn.shape[position]) // (drawn.shape[position] // blocks)).reshape((-1,) + (1,) * (drawn.ndim - 1 - position))

    first = jax.random.permutation(stream_key, blocks)[block_of(target)]
    other_side = (block_of(target) + blocks // 2) % blocks
    return jnp.where((block_of(source) == first) | (block_of(source) == other_side), factor * drawn, drawn)


def block_levels(stream_key, shape, cuts, low, largest):
    level, own = 1.0, jax.random.fold_in(stream_key, 6)
    for position, parts in cuts:
        steps = jnp.exp(jax.random.uniform(jax.random.fold_in(own, position), (parts,), jnp.float32, low / len(cuts), largest / len(cuts)))
        level = level * jnp.repeat(steps, shape[position] // parts).reshape([-1 if axis == position else 1 for axis in range(len(shape))])
    return level


def bell_draw(own_key, extent, deviation, bound, pieces=(), dtype=jnp.bfloat16):
    entries = jax.random.normal(own_key, extent, jnp.float32) * deviation
    if len(pieces) > 0:
        entries = block_levels(own_key, extent, pieces, -0.22, 0.18) * entries
    return jnp.clip(entries, min=-bound, max=bound).astype(dtype)


def noise_with(key, shape, scale, most, shards, heavy, kind=jnp.bfloat16):
    array = scale * jax.random.normal(key, shape, jnp.float32)
    if shards:
        array = array * block_levels(key, shape, shards, -0.22, 0.18)
    return jnp.clip(strengthened(array, jax.random.fold_in(key, 3), *heavy), -most, most).astype(kind)


def setup_inputs(seed: int = 0) -> dict:
    arg_keys = jax.random.split(jax.random.key(seed), 10)
    return {
        "tokens": noise_with(arg_keys[0], (TOKENS, D), 1.0, 6.0, ((0, 32),), (0, 1, 32, 2.75)),
        "cotangent": bell_draw(arg_keys[1], (TOKENS, HD), ((TOK_DEV * N_FSDP) ** -0.5), 0.09375, ((0, 32),)),
        "keep_mask": place_ends((jax.random.randint(arg_keys[2], (TOKENS,), 0, 4) < 3).astype(jnp.int32), jax.random.fold_in(arg_keys[2], 1), 0, 1),
        "key_weight": bell_draw(arg_keys[3], (REPLICAS, D, HD), D ** -0.5, 0.0625, ((0, 2), (1, 16))),
        "norm_gain": jnp.clip(1.0 + 0.18 * jax.random.normal(arg_keys[4], (REPLICAS, D), jnp.float32), 0.1, 1.9),
        "local_params": draw_local_params(jax.random.fold_in(arg_keys[9], 71), 0),
        "global_params": draw_global_params(jax.random.fold_in(arg_keys[9], 71), 0),
        "momentum": bell_draw(arg_keys[7], (HELD, P_ALL), 1.0, 6.0, ((1, 16),), jnp.float32),
        "fragment_order": jax.random.permutation(arg_keys[8], HELD).astype(jnp.int32),
    }


EPSILON = 1e-06
CLIP_RATE = 0.5
MOMENT = 0.9
OUTER_RATE = 0.7
MIX_RATE = 0.5

def group_grads(inputs):
    rows, cot_rows, mask_rows, weight, gain = inputs
    as_float = rows.astype(jnp.float32)
    inv_rms = lax.rsqrt(lax.optimization_barrier(jnp.mean(as_float * as_float, axis=1, keepdims=True)) + EPSILON)
    unit_rows = as_float * inv_rms
    normed = unit_rows.astype(jnp.bfloat16)
    masked = jnp.where(mask_rows[:, None] == 1, cot_rows, jnp.zeros_like(cot_rows))
    weight_grad = gain[:, None] * jnp.dot(normed.T, masked, preferred_element_type=jnp.float32)
    hidden_grad = jnp.dot(masked, weight.T, preferred_element_type=jnp.float32)
    gain_grad = lax.optimization_barrier(jnp.sum(hidden_grad * unit_rows, axis=0))
    return (weight_grad, gain_grad)

def reference(tokens, cotangent, keep_mask, key_weight, norm_gain, local_params, global_params, momentum, fragment_order):
    group = TOK_DEV * N_FSDP
    tok_groups = tokens.reshape(REPLICAS, group, D)
    cot_groups = cotangent.reshape(REPLICAS, group, HD)
    mask_groups = keep_mask.reshape(REPLICAS, group)
    weight_grad, gain_grad = lax.map(group_grads, (tok_groups, cot_groups, mask_groups, key_weight, norm_gain))
    frag_rows = fragment_order[:FRAG]
    local_rows = jnp.take(local_params, frag_rows, axis=1)
    glob_rows = jnp.take(global_params, frag_rows, axis=0)
    moment_rows = jnp.take(momentum, frag_rows, axis=0)
    delta = glob_rows[None] - local_rows
    averaged = lax.optimization_barrier(jnp.sum(delta, axis=0)) / REPLICAS
    squares = jnp.sum(averaged * averaged)
    limit = CLIP_RATE * jnp.sqrt(jnp.float32(FRAG * P_ALL))
    factor = jnp.minimum(1.0, limit / jnp.sqrt(squares + EPSILON))
    clipped = averaged * factor
    moment_new = MOMENT * moment_rows + clipped
    global_new = glob_rows - OUTER_RATE * (clipped + MOMENT * moment_new)
    merged = MIX_RATE * local_rows + (1.0 - MIX_RATE) * global_new[None]
    local_out = local_params.at[:, frag_rows].set(merged)
    global_out = global_params.at[frag_rows].set(global_new)
    moment_out = momentum.at[frag_rows].set(moment_new)
    return (weight_grad, gain_grad, local_out, global_out, moment_out)
```

```python
import functools

import jax
import jax.numpy as jnp
from jax import lax
from jax.experimental import pallas as pl
from jax.experimental.pallas import tpu as pltpu
from jax.sharding import PartitionSpec as P

FRAG = 2


EPSILON = 1e-06
CLIP_RATE = 0.5
MOMENT = 0.9
OUTER_RATE = 0.7
MIX_RATE = 0.5

LANES = 128
PACKED_ROWS = 16
ROW_BLOCK = 32
MIB = 1024 * 1024


def fsdp_factors(count):
    factors = []
    for factor in (2, 2):
        if count % factor == 0:
            factors.append(factor)
            count //= factor
    while count % 4 == 0:
        factors.append(4)
        count //= 4
    while count % 2 == 0:
        factors.append(2)
        count //= 2
    assert count == 1
    return factors


def xor_pairs(count, mask):
    return [(i, i ^ mask) for i in range(count)]


def swap(array, mask):
    return lax.ppermute(array, "fsdp", xor_pairs(lax.axis_size("fsdp"), mask))


def cross_swap(array, even, odd):
    count = lax.axis_size("fsdp")
    return lax.ppermute(array, "fsdp", [(i, i ^ (odd if i % 2 else even)) for i in range(count)])


VMEM = pl.BlockSpec(memory_space=pltpu.VMEM)
SMEM = pl.BlockSpec(memory_space=pltpu.SMEM)
HBM = pl.BlockSpec(memory_space=pltpu.HBM)
ANY = pl.BlockSpec(memory_space=pl.ANY)


def local_call(kernel, name, outs, in_specs, vmem_mib, scratch=(), out_spec=VMEM, moved=0, aliases=None):
    return pl.pallas_call(
        kernel,
        name=name,
        out_shape=[jax.ShapeDtypeStruct(shape, dtype) for shape, dtype in outs],
        in_specs=in_specs,
        out_specs=[out_spec] * len(outs),
        scratch_shapes=list(scratch),
        input_output_aliases=aliases or {},
        cost_estimate=pl.CostEstimate(flops=0, bytes_accessed=moved, transcendentals=0),
        compiler_params=pltpu.CompilerParams(vmem_limit_bytes=vmem_mib * MIB),
    )


def in_hbm(array):
    return pltpu.with_memory_space_constraint(array, pltpu.HBM)


def squares_tile(squares):
    value = squares[0:1, :]
    pieces = []
    for _ in range(3):
        piece = value.astype(jnp.bfloat16).astype(jnp.float32)
        pieces.append(piece)
        value = value - piece
    pieces.append(jnp.zeros((PACKED_ROWS - 3, LANES), jnp.float32))
    return jnp.concatenate(pieces, axis=0).astype(jnp.bfloat16)


def tile_squares(tile):
    tile = tile.astype(jnp.float32)
    return (tile[0:1] + tile[1:2]) + tile[2:3]


def rows_kernel(tokens, cotangent, mask, order, local_params, global_params, held, left, delta, squares, cot, keep, at, own, shared, sems, more):
    rows, width = held.shape
    blocks = rows // ROW_BLOCK
    copies = []
    small = [
        pltpu.make_async_copy(source, target, more.at[i])
        for i, (source, target) in enumerate(
            ((order, at), (global_params, shared), (local_params, own), (cotangent, cot), (mask, keep))
        )
    ]
    small[0].start()
    for i in range(blocks):
        here = pl.ds(i * ROW_BLOCK, ROW_BLOCK)
        copies.append(pltpu.make_async_copy(tokens.at[here], held.at[here], sems.at[i]))
        copies[-1].start()
        if i == 0:
            for copy in small[1:]:
                copy.start()
    for i, copy in enumerate(copies):
        if i == blocks // 2:
            for other in small:
                other.wait()
            picked = []
            for j in range(FRAG):
                row = pl.ds(at[j], 1)
                picked.append(shared[row, :] - own[0, row, :])
            delta[...] = jnp.concatenate(picked, axis=0).astype(jnp.bfloat16)
            cot_t = cot[...].astype(jnp.float32).T
        copy.wait()
        here = pl.ds(i * ROW_BLOCK, ROW_BLOCK)
        totals = [jnp.zeros((ROW_BLOCK, LANES), jnp.float32)] * 4
        for j in range(width // LANES):
            part = held[here, j * LANES : (j + 1) * LANES].astype(jnp.float32)
            totals[j % 4] = totals[j % 4] + part * part
        squares[here, :] = (totals[0] + totals[1]) + (totals[2] + totals[3])
    mean = jnp.sum(squares[...].T, axis=0, keepdims=True) * (1.0 / width)
    scale = jnp.where(keep[...] == 1, lax.rsqrt(mean + EPSILON), 0.0)
    scaled = cot_t * scale
    high = scaled.astype(jnp.bfloat16)
    low = (scaled - high.astype(jnp.float32)).astype(jnp.bfloat16)
    left[...] = jnp.concatenate([high, low], axis=0)


def place_bits():
    index = lax.axis_index("fsdp")
    core = lax.rem(index, 2)
    y = lax.rem(index // 2, 2)
    near = lax.rem(index // 4, 2)
    straight = core == 0
    return straight, jnp.where(straight, y, near), jnp.where(straight, near, y)


def partial_kernel(tiles, own_half, held, left, send, keep):
    heads = send.shape[2]
    chunk = tiles * PACKED_ROWS
    index = lax.axis_index("fsdp")
    first = lax.rem(index, 2) == 0
    half = index // 8 if own_half else 1 - index // 8
    for k in range(4):
        start = pl.multiple_of(half * (8 * chunk) + k * 2 * chunk, LANES)
        both = jnp.dot(
            left[...], held[:, pl.ds(start, 2 * chunk)], preferred_element_type=jnp.float32
        )
        sums = (both[:heads] + both[heads:]).T.reshape(2, tiles, PACKED_ROWS, heads)
        here = slice(k * tiles, (k + 1) * tiles)
        send[here] = jnp.where(first, sums[1], sums[0]).astype(jnp.bfloat16)
        keep[here] = jnp.where(first, sums[0], sums[1])


def spread_kernel(gain, after, spread):
    spread[...] = jnp.broadcast_to(gain[...], spread.shape[::-1]).T


def squares_kernel(own, other, after, squares):
    mean = (own[...].astype(jnp.float32) + other[...].astype(jnp.float32)) * 0.5
    squares[...] = jnp.broadcast_to(jnp.sum(mean * mean), squares.shape)


def pass_squares(squares, came, send, squares_sum):
    both = squares[...] + tile_squares(came[came.shape[0] - 1])
    squares_sum[...] = both
    if send is not None:
        send[send.shape[0] - 1] = squares_tile(both)


def first_kernel(keep, came, *rest):
    tiles = keep.shape[0] // 4
    straight, own, _ = place_bits()
    if len(rest) == 5:
        squares, squares_came, send, kept, squares_sum = rest
        both = squares[...] + squares_came[...]
        squares_sum[...] = both
        send[2 * tiles] = squares_tile(both)
    else:
        send, kept = rest

    def total(bit, other):
        place = jnp.where(straight, bit + 2 * other, 2 * bit + other)
        there = pl.ds(place * tiles, tiles)
        return keep[there] + came[there].astype(jnp.float32)

    for other in range(2):
        here = slice(other * tiles, (other + 1) * tiles)
        send[here] = total(1 - own, other).astype(jnp.bfloat16)
        kept[here] = total(own, other)


def first_far_kernel(keep, came, after, passing, send, kept, passed):
    first_kernel(keep, came, send, kept)


def second_kernel(keep, came, *rest):
    squares, send, kept, squares_sum = rest if len(rest) == 4 else (None, *rest, None)
    tiles = keep.shape[0] // 2
    _, _, own = place_bits()
    if squares is not None:
        pass_squares(squares, came, send, squares_sum)

    def total(bit):
        there = pl.ds(bit * tiles, tiles)
        return keep[there] + came[there].astype(jnp.float32)

    send[:tiles] = total(1 - own).astype(jnp.bfloat16)
    kept[...] = total(own)


def third_kernel(keep, came, squares, send):
    tiles = keep.shape[0]
    send[:tiles] = (keep[...] + came[...].astype(jnp.float32)).astype(jnp.bfloat16)
    send[tiles] = squares_tile(squares[...])


def prepare_kernel(keep, came, squares, order, own, other, local_params, global_params, momentum, kept, squares_sum, local_base, global_base, moment_base, local_slope, global_slope, moment_slope):
    pass_squares(squares, came, None, squares_sum)
    kept[...] = keep[...] + came[: keep.shape[0]].astype(jnp.float32)
    local_base[...] = local_params[...]
    global_base[...] = global_params[...]
    moment_base[...] = momentum[...]
    for slope in (local_slope, global_slope, moment_slope):
        slope[...] = jnp.zeros_like(slope)
    mean = (own[...].astype(jnp.float32) + other[...].astype(jnp.float32)) * 0.5
    for i in range(FRAG):
        row = pl.ds(order[i], 1)
        averaged = mean[i : i + 1, :]
        moment_kept = MOMENT * momentum[row, :]
        global_kept = global_params[row, :] - OUTER_RATE * MOMENT * moment_kept
        global_step = -(OUTER_RATE * (1.0 + MOMENT)) * averaged
        moment_base[row, :] = moment_kept
        moment_slope[row, :] = averaged
        global_base[row, :] = global_kept
        global_slope[row, :] = global_step
        local_base[0, row, :] = MIX_RATE * local_params[0, row, :] + (1.0 - MIX_RATE) * global_kept
        local_slope[0, row, :] = (1.0 - MIX_RATE) * global_step


def last_kernel(count, keep, came, squares, squares_came, weight, spread, local_base, global_base, moment_base, local_slope, global_slope, moment_slope, weight_grad, gain_grad, local_out, global_out, moment_out, grad_held, gain_held, local_held, global_held, moment_held, sems):
    tiles = keep.shape[0]
    copies = []

    def put(source, target):
        copies.append(pltpu.make_async_copy(source, target, sems.at[len(copies)]))
        copies[-1].start()

    grad = (keep[...] + came[:tiles].astype(jnp.float32)).reshape(weight.shape[1:])
    grad_held[0] = grad * spread[...]
    put(grad_held, weight_grad)
    total = squares[0:1, :] + (tile_squares(came[tiles]) + squares_came[0:1, :])
    limit = CLIP_RATE * count**0.5
    factor = jnp.minimum(1.0, limit / jnp.sqrt(total[:, 0:1] + EPSILON))
    local_held[0] = local_base[0] + factor * local_slope[0]
    put(local_held, local_out)
    global_held[...] = global_base[...] + factor * global_slope[...]
    put(global_held, global_out)
    moment_held[...] = moment_base[...] + factor * moment_slope[...]
    put(moment_held, moment_out)
    products = (grad * weight[0].astype(jnp.float32)).T
    gain_held[...] = jnp.sum(products, axis=0, keepdims=True)
    put(gain_held, gain_grad)
    for copy in copies:
        copy.wait()


def three_stage(tokens, cotangent, keep_mask, key_weight, norm_gain, local_params, global_params, momentum, fragment_order):
    rows, features = tokens.shape
    chunk, heads = key_weight.shape[1:]
    tiles = chunk // PACKED_ROWS
    width = global_params.shape[1]
    bf16, f32 = jnp.bfloat16, jnp.float32
    row_sum = ((8, LANES), f32)

    def blocks(count, dtype):
        return ((count, PACKED_ROWS, heads), dtype)

    held, left, delta = local_call(
        rows_kernel,
        "token_rows",
        [((rows, features), bf16), ((2 * heads, rows), bf16), ((FRAG, width), bf16)],
        [HBM] * 6,
        24,
        [
            pltpu.VMEM((rows, LANES), f32),
            pltpu.VMEM((rows, heads), bf16),
            pltpu.VMEM((1, rows), jnp.int32),
            pltpu.SMEM(fragment_order.shape, jnp.int32),
            pltpu.VMEM(local_params.shape, f32),
            pltpu.VMEM(global_params.shape, f32),
            pltpu.SemaphoreType.DMA((rows // ROW_BLOCK,)),
            pltpu.SemaphoreType.DMA((5,)),
        ],
    )(*map(in_hbm, (tokens, cotangent, keep_mask[None], fragment_order, local_params, global_params)))
    other = lax.ppermute(delta, "replica", [(0, 1), (1, 0)])

    def partial(own_half):
        return local_call(
            functools.partial(partial_kernel, tiles, own_half),
            "partial_own" if own_half else "partial_far",
            [blocks(4 * tiles, bf16), blocks(4 * tiles, f32)],
            [VMEM] * 2,
            16,
            moved=4 * MIB,
        )(held, left)

    far_send, far_keep = partial(False)
    far_came = swap(far_send, 1)
    own_send, own_keep = partial(True)

    far_send, far_keep, own_send = local_call(
        first_far_kernel,
        "first_far",
        [blocks(2 * tiles, bf16), blocks(2 * tiles, f32), blocks(4 * tiles, bf16)],
        [VMEM] * 2 + [ANY, VMEM],
        8,
        aliases={3: 2},
    )(far_keep, far_came, other, pltpu.with_memory_space_constraint(own_send, pltpu.VMEM))
    far_came = cross_swap(far_send, 2, 4)
    own_came = swap(own_send, 1)

    (spread,) = local_call(
        spread_kernel, "gain_spread", [((chunk, heads), f32)], [VMEM, ANY], 4, moved=8 * MIB
    )(norm_gain, far_send)
    (squares,) = local_call(
        squares_kernel, "squares", [row_sum], [VMEM] * 2 + [ANY], 4
    )(delta, other, spread)
    squares_came = swap(squares, 1)
    own_send, own_keep, squares = local_call(
        first_kernel, "first_own", [blocks(2 * tiles + 1, bf16), blocks(2 * tiles, f32), row_sum], [VMEM] * 4, 8
    )(own_keep, own_came, squares, squares_came)
    own_came = cross_swap(own_send, 2, 4)

    far_send, far_keep = local_call(
        second_kernel, "second_far", [blocks(tiles, bf16), blocks(tiles, f32)], [VMEM] * 2, 8
    )(far_keep, far_came)
    far_came = cross_swap(far_send, 4, 2)
    own_send, own_keep, squares = local_call(
        second_kernel, "second_own", [blocks(tiles + 1, bf16), blocks(tiles, f32), row_sum], [VMEM] * 3, 8
    )(own_keep, own_came, squares)
    own_came = cross_swap(own_send, 4, 2)

    (far_send,) = local_call(
        third_kernel, "third_far", [blocks(tiles + 1, bf16)], [VMEM] * 3, 8
    )(far_keep, far_came, squares)
    far_came = swap(far_send, 8)
    squares_came = cross_swap(squares, 12, 10)

    states = [(local_params.shape, f32), (global_params.shape, f32), (momentum.shape, f32)]
    own_keep, squares, *parts = local_call(
        prepare_kernel,
        "prepare_ends",
        [blocks(tiles, f32), row_sum] + states + states,
        [VMEM] * 3 + [SMEM] + [VMEM] * 5,
        8,
    )(own_keep, own_came, squares, fragment_order, delta, other, local_params, global_params, momentum)

    count = FRAG * width * lax.axis_size("fsdp")
    return local_call(
        functools.partial(last_kernel, count),
        "both_ends",
        [((1, chunk, heads), f32), ((1, chunk), f32)] + states,
        [VMEM] * 12,
        8,
        [pltpu.VMEM((1, chunk, heads), f32), pltpu.VMEM((1, chunk), f32)]
        + [pltpu.VMEM(shape, dtype) for shape, dtype in states]
        + [pltpu.SemaphoreType.DMA((5,))],
        HBM,
    )(own_keep, far_came, squares, squares_came, key_weight, spread, *parts)


def scatter_sum(partial):
    count = lax.axis_size("fsdp")
    factors = fsdp_factors(count)
    place = lax.axis_index("fsdp")
    rest = partial.reshape(tuple(reversed(factors)) + (partial.shape[0] // count, partial.shape[1]))
    stride = 1
    for factor in factors:
        axis = rest.ndim - 3
        own = (place // stride) % factor
        arrived = []
        for offset in range(1, factor):
            block = lax.dynamic_index_in_dim(rest, own ^ offset, axis, keepdims=False)
            arrived.append(swap(block.astype(jnp.bfloat16), offset * stride))
        total = lax.dynamic_index_in_dim(rest, own, axis, keepdims=False)
        for block in arrived:
            total = total + block.astype(jnp.float32)
        rest = total
        stride *= factor
    return rest


def scalar_sum(value):
    count = lax.axis_size("fsdp")
    mask = 1
    while mask < count:
        value = value + swap(value, mask)
        mask *= 2
    return value


def outer_step(averaged, glob_rows, moment_rows, squares, count):
    limit = CLIP_RATE * jnp.sqrt(jnp.float32(count))
    factor = jnp.minimum(1.0, limit / jnp.sqrt(squares + EPSILON))
    clipped = averaged * factor
    moment_new = MOMENT * moment_rows + clipped
    global_new = glob_rows - OUTER_RATE * (clipped + MOMENT * moment_new)
    return (moment_new, global_new)


def inner_part(tokens, cotangent, keep_mask, key_weight, norm_gain):
    as_float = tokens.astype(jnp.float32)
    inv_rms = lax.rsqrt(jnp.mean(as_float * as_float, axis=1, keepdims=True) + EPSILON)
    unit_rows = as_float * inv_rms
    normed = unit_rows.astype(jnp.bfloat16)
    masked = jnp.where(keep_mask[:, None] == 1, cotangent, jnp.zeros_like(cotangent))
    partial_grad = jnp.einsum("td,th->dh", normed, masked, preferred_element_type=jnp.float32)
    own_grad = scatter_sum(partial_grad)
    gain_grad = jnp.sum(own_grad * key_weight[0].astype(jnp.float32), axis=1)
    weight_grad = (norm_gain[0][:, None] * own_grad)[None]
    return (weight_grad, gain_grad[None])


def outer_part(local_params, global_params, momentum, fragment_order):
    frag_rows = fragment_order[:FRAG]
    own_local = local_params[0]
    local_rows = jnp.take(own_local, frag_rows, axis=0)
    glob_rows = jnp.take(global_params, frag_rows, axis=0)
    moment_rows = jnp.take(momentum, frag_rows, axis=0)
    delta = glob_rows - local_rows
    replicas = lax.axis_size("replica")
    count = FRAG * global_params.shape[1] * lax.axis_size("fsdp")
    gathered = lax.all_gather(delta.astype(jnp.bfloat16), "replica", axis=0)
    averaged = jnp.sum(gathered.astype(jnp.float32), axis=0) / replicas
    squares = scalar_sum(jnp.sum(averaged * averaged))
    moment_new, global_new = outer_step(averaged, glob_rows, moment_rows, squares, count)
    merged = MIX_RATE * local_rows + (1.0 - MIX_RATE) * global_new
    local_out = own_local.at[frag_rows].set(merged)[None]
    global_out = global_params.at[frag_rows].set(global_new)
    moment_out = momentum.at[frag_rows].set(moment_new)
    return (local_out, global_out, moment_out)


def per_device(
    tokens,
    cotangent,
    keep_mask,
    key_weight,
    norm_gain,
    local_params,
    global_params,
    momentum,
    fragment_order,
):
    chunk = key_weight.shape[1]
    three_stages = fsdp_factors(lax.axis_size("fsdp")) == [2, 2, 4]
    aligned = chunk % PACKED_ROWS == 0 and (2 * chunk) % LANES == 0
    if three_stages and aligned and lax.axis_size("replica") == 2:
        return three_stage(
            tokens,
            cotangent,
            keep_mask,
            key_weight,
            norm_gain,
            local_params,
            global_params,
            momentum,
            fragment_order,
        )
    weight_grad, gain_grad = inner_part(tokens, cotangent, keep_mask, key_weight, norm_gain)
    local_out, global_out, moment_out = outer_part(
        local_params, global_params, momentum, fragment_order
    )
    return (weight_grad, gain_grad, local_out, global_out, moment_out)


def solution(mesh):
    in_specs = (
        P(("replica", "fsdp"), None),
        P(("replica", "fsdp"), None),
        P(("replica", "fsdp")),
        P("replica", "fsdp", None),
        P("replica", "fsdp"),
        P("replica", None, "fsdp"),
        P(None, "fsdp"),
        P(None, "fsdp"),
        P(),
    )
    out_specs = (
        P("replica", "fsdp", None),
        P("replica", "fsdp"),
        P("replica", None, "fsdp"),
        P(None, "fsdp"),
        P(None, "fsdp"),
    )
    return jax.shard_map(
        per_device, mesh=mesh, in_specs=in_specs, out_specs=out_specs, check_vma=False
    )
```

```python
import functools

import jax
import jax.numpy as jnp
from jax import lax
from jax.experimental import pallas as pl
from jax.experimental.pallas import tpu as pltpu
from jax.sharding import PartitionSpec as P

FRAG = 2


EPSILON = 1e-06
CLIP_RATE = 0.5
MOMENT = 0.9
OUTER_RATE = 0.7
MIX_RATE = 0.5

LANES = 128
PACKED_ROWS = 16
ROW_BLOCK = 32
MIB = 1024 * 1024


def fsdp_factors(count):
    factors = []
    for factor in (2, 2):
        if count % factor == 0:
            factors.append(factor)
            count //= factor
    while count % 4 == 0:
        factors.append(4)
        count //= 4
    while count % 2 == 0:
        factors.append(2)
        count //= 2
    assert count == 1
    return factors


def xor_pairs(count, mask):
    return [(i, i ^ mask) for i in range(count)]


def swap(array, mask):
    return lax.ppermute(array, "fsdp", xor_pairs(lax.axis_size("fsdp"), mask))


def cross_swap(array, even, odd):
    count = lax.axis_size("fsdp")
    return lax.ppermute(array, "fsdp", [(i, i ^ (odd if i % 2 else even)) for i in range(count)])


VMEM = pl.BlockSpec(memory_space=pltpu.VMEM)
SMEM = pl.BlockSpec(memory_space=pltpu.SMEM)
HBM = pl.BlockSpec(memory_space=pltpu.HBM)
ANY = pl.BlockSpec(memory_space=pl.ANY)


def local_call(kernel, name, outs, in_specs, vmem_mib, scratch=(), out_spec=VMEM, moved=0, aliases=None):
    return pl.pallas_call(
        kernel,
        name=name,
        out_shape=[jax.ShapeDtypeStruct(shape, dtype) for shape, dtype in outs],
        in_specs=in_specs,
        out_specs=[out_spec] * len(outs),
        scratch_shapes=list(scratch),
        input_output_aliases=aliases or {},
        cost_estimate=pl.CostEstimate(flops=0, bytes_accessed=moved, transcendentals=0),
        compiler_params=pltpu.CompilerParams(vmem_limit_bytes=vmem_mib * MIB),
    )


def in_hbm(array):
    return pltpu.with_memory_space_constraint(array, pltpu.HBM)


def squares_tile(squares):
    value = squares[0:1, :]
    pieces = []
    for _ in range(3):
        piece = value.astype(jnp.bfloat16).astype(jnp.float32)
        pieces.append(piece)
        value = value - piece
    pieces.append(jnp.zeros((PACKED_ROWS - 3, LANES), jnp.float32))
    return jnp.concatenate(pieces, axis=0).astype(jnp.bfloat16)


def tile_squares(tile):
    tile = tile.astype(jnp.float32)
    return (tile[0:1] + tile[1:2]) + tile[2:3]


def rows_kernel(tokens, cotangent, mask, order, local_params, global_params, held, left, delta, squares, cot, keep, at, own, shared, sems, more):
    rows, width = held.shape
    blocks = rows // ROW_BLOCK
    copies = []
    small = [
        pltpu.make_async_copy(source, target, more.at[i])
        for i, (source, target) in enumerate(
            ((order, at), (global_params, shared), (local_params, own), (cotangent, cot), (mask, keep))
        )
    ]
    small[0].start()
    for i in range(blocks):
        here = pl.ds(i * ROW_BLOCK, ROW_BLOCK)
        copies.append(pltpu.make_async_copy(tokens.at[here], held.at[here], sems.at[i]))
        copies[-1].start()
        if i == 0:
            for copy in small[1:]:
                copy.start()
    for i, copy in enumerate(copies):
        if i == blocks // 2:
            for other in small:
                other.wait()
            picked = []
            for j in range(FRAG):
                row = pl.ds(at[j], 1)
                picked.append(shared[row, :] - own[0, row, :])
            delta[...] = jnp.concatenate(picked, axis=0).astype(jnp.bfloat16)
            cot_t = cot[...].astype(jnp.float32).T
        copy.wait()
        here = pl.ds(i * ROW_BLOCK, ROW_BLOCK)
        totals = [jnp.zeros((ROW_BLOCK, LANES), jnp.float32)] * 4
        for j in range(width // LANES):
            part = held[here, j * LANES : (j + 1) * LANES].astype(jnp.float32)
            totals[j % 4] = totals[j % 4] + part * part
        squares[here, :] = (totals[0] + totals[1]) + (totals[2] + totals[3])
    mean = jnp.sum(squares[...].T, axis=0, keepdims=True) * (1.0 / width)
    scale = jnp.where(keep[...] == 1, lax.rsqrt(mean + EPSILON), 0.0)
    scaled = cot_t * scale
    left[...] = scaled.astype(jnp.bfloat16)


def place_bits():
    index = lax.axis_index("fsdp")
    core = lax.rem(index, 2)
    y = lax.rem(index // 2, 2)
    near = lax.rem(index // 4, 2)
    straight = core == 0
    return straight, jnp.where(straight, y, near), jnp.where(straight, near, y)


def partial_kernel(tiles, own_half, held, left, send, keep):
    heads = send.shape[2]
    chunk = tiles * PACKED_ROWS
    index = lax.axis_index("fsdp")
    first = lax.rem(index, 2) == 0
    half = index // 8 if own_half else 1 - index // 8
    for k in range(4):
        start = pl.multiple_of(half * (8 * chunk) + k * 2 * chunk, LANES)
        both = jnp.dot(
            left[...], held[:, pl.ds(start, 2 * chunk)], preferred_element_type=jnp.float32
        )
        sums = both.T.reshape(2, tiles, PACKED_ROWS, heads)
        here = slice(k * tiles, (k + 1) * tiles)
        send[here] = jnp.where(first, sums[1], sums[0]).astype(jnp.bfloat16)
        keep[here] = jnp.where(first, sums[0], sums[1])


def spread_kernel(gain, after, spread):
    spread[...] = jnp.broadcast_to(gain[...], spread.shape[::-1]).T


def squares_kernel(own, other, after, squares):
    mean = (own[...].astype(jnp.float32) + other[...].astype(jnp.float32)) * 0.5
    squares[...] = jnp.broadcast_to(jnp.sum(mean * mean), squares.shape)


def pass_squares(squares, came, send, squares_sum):
    both = squares[...] + tile_squares(came[came.shape[0] - 1])
    squares_sum[...] = both
    if send is not None:
        send[send.shape[0] - 1] = squares_tile(both)


def first_kernel(keep, came, *rest):
    tiles = keep.shape[0] // 4
    straight, own, _ = place_bits()
    if len(rest) == 5:
        squares, squares_came, send, kept, squares_sum = rest
        both = squares[...] + squares_came[...]
        squares_sum[...] = both
        send[2 * tiles] = squares_tile(both)
    else:
        send, kept = rest

    def total(bit, other):
        place = jnp.where(straight, bit + 2 * other, 2 * bit + other)
        there = pl.ds(place * tiles, tiles)
        return keep[there] + came[there].astype(jnp.float32)

    for other in range(2):
        here = slice(other * tiles, (other + 1) * tiles)
        send[here] = total(1 - own, other).astype(jnp.bfloat16)
        kept[here] = total(own, other)


def first_far_kernel(keep, came, after, passing, send, kept, passed):
    first_kernel(keep, came, send, kept)


def second_kernel(keep, came, *rest):
    squares, send, kept, squares_sum = rest if len(rest) == 4 else (None, *rest, None)
    tiles = keep.shape[0] // 2
    _, _, own = place_bits()
    if squares is not None:
        pass_squares(squares, came, send, squares_sum)

    def total(bit):
        there = pl.ds(bit * tiles, tiles)
        return keep[there] + came[there].astype(jnp.float32)

    send[:tiles] = total(1 - own).astype(jnp.bfloat16)
    kept[...] = total(own)


def third_kernel(keep, came, squares, send):
    tiles = keep.shape[0]
    send[:tiles] = (keep[...] + came[...].astype(jnp.float32)).astype(jnp.bfloat16)
    send[tiles] = squares_tile(squares[...])


def prepare_kernel(keep, came, squares, order, own, other, local_params, global_params, momentum, kept, squares_sum, local_base, global_base, moment_base, local_slope, global_slope, moment_slope):
    pass_squares(squares, came, None, squares_sum)
    kept[...] = keep[...] + came[: keep.shape[0]].astype(jnp.float32)
    local_base[...] = local_params[...]
    global_base[...] = global_params[...]
    moment_base[...] = momentum[...]
    for slope in (local_slope, global_slope, moment_slope):
        slope[...] = jnp.zeros_like(slope)
    mean = (own[...].astype(jnp.float32) + other[...].astype(jnp.float32)) * 0.5
    for i in range(FRAG):
        row = pl.ds(order[i], 1)
        averaged = mean[i : i + 1, :]
        moment_kept = MOMENT * momentum[row, :]
        global_kept = global_params[row, :] - OUTER_RATE * MOMENT * moment_kept
        global_step = -(OUTER_RATE * (1.0 + MOMENT)) * averaged
        moment_base[row, :] = moment_kept
        moment_slope[row, :] = averaged
        global_base[row, :] = global_kept
        global_slope[row, :] = global_step
        local_base[0, row, :] = MIX_RATE * local_params[0, row, :] + (1.0 - MIX_RATE) * global_kept
        local_slope[0, row, :] = (1.0 - MIX_RATE) * global_step


def last_kernel(count, keep, came, squares, squares_came, weight, spread, local_base, global_base, moment_base, local_slope, global_slope, moment_slope, weight_grad, gain_grad, local_out, global_out, moment_out, grad_held, gain_held, local_held, global_held, moment_held, sems):
    tiles = keep.shape[0]
    copies = []

    def put(source, target):
        copies.append(pltpu.make_async_copy(source, target, sems.at[len(copies)]))
        copies[-1].start()

    grad = (keep[...] + came[:tiles].astype(jnp.float32)).reshape(weight.shape[1:])
    grad_held[0] = grad * spread[...]
    put(grad_held, weight_grad)
    total = squares[0:1, :] + (tile_squares(came[tiles]) + squares_came[0:1, :])
    limit = CLIP_RATE * count**0.5
    factor = jnp.minimum(1.0, limit / jnp.sqrt(total[:, 0:1] + EPSILON))
    local_held[0] = local_base[0] + factor * local_slope[0]
    put(local_held, local_out)
    global_held[...] = global_base[...] + factor * global_slope[...]
    put(global_held, global_out)
    moment_held[...] = moment_base[...] + factor * moment_slope[...]
    put(moment_held, moment_out)
    products = (grad * weight[0].astype(jnp.float32)).T
    gain_held[...] = jnp.sum(products, axis=0, keepdims=True)
    put(gain_held, gain_grad)
    for copy in copies:
        copy.wait()


def three_stage(tokens, cotangent, keep_mask, key_weight, norm_gain, local_params, global_params, momentum, fragment_order):
    rows, features = tokens.shape
    chunk, heads = key_weight.shape[1:]
    tiles = chunk // PACKED_ROWS
    width = global_params.shape[1]
    bf16, f32 = jnp.bfloat16, jnp.float32
    row_sum = ((8, LANES), f32)

    def blocks(count, dtype):
        return ((count, PACKED_ROWS, heads), dtype)

    held, left, delta = local_call(
        rows_kernel,
        "token_rows",
        [((rows, features), bf16), ((heads, rows), bf16), ((FRAG, width), bf16)],
        [HBM] * 6,
        24,
        [
            pltpu.VMEM((rows, LANES), f32),
            pltpu.VMEM((rows, heads), bf16),
            pltpu.VMEM((1, rows), jnp.int32),
            pltpu.SMEM(fragment_order.shape, jnp.int32),
            pltpu.VMEM(local_params.shape, f32),
            pltpu.VMEM(global_params.shape, f32),
            pltpu.SemaphoreType.DMA((rows // ROW_BLOCK,)),
            pltpu.SemaphoreType.DMA((5,)),
        ],
    )(*map(in_hbm, (tokens, cotangent, keep_mask[None], fragment_order, local_params, global_params)))
    other = lax.ppermute(delta, "replica", [(0, 1), (1, 0)])

    def partial(own_half):
        return local_call(
            functools.partial(partial_kernel, tiles, own_half),
            "partial_own" if own_half else "partial_far",
            [blocks(4 * tiles, bf16), blocks(4 * tiles, f32)],
            [VMEM] * 2,
            16,
            moved=4 * MIB,
        )(held, left)

    far_send, far_keep = partial(False)
    far_came = swap(far_send, 1)
    own_send, own_keep = partial(True)

    far_send, far_keep, own_send = local_call(
        first_far_kernel,
        "first_far",
        [blocks(2 * tiles, bf16), blocks(2 * tiles, f32), blocks(4 * tiles, bf16)],
        [VMEM] * 2 + [ANY, VMEM],
        8,
        aliases={3: 2},
    )(far_keep, far_came, other, pltpu.with_memory_space_constraint(own_send, pltpu.VMEM))
    far_came = cross_swap(far_send, 2, 4)
    own_came = swap(own_send, 1)

    (spread,) = local_call(
        spread_kernel, "gain_spread", [((chunk, heads), f32)], [VMEM, ANY], 4, moved=8 * MIB
    )(norm_gain, far_send)
    (squares,) = local_call(
        squares_kernel, "squares", [row_sum], [VMEM] * 2 + [ANY], 4
    )(delta, other, spread)
    squares_came = swap(squares, 1)
    own_send, own_keep, squares = local_call(
        first_kernel, "first_own", [blocks(2 * tiles + 1, bf16), blocks(2 * tiles, f32), row_sum], [VMEM] * 4, 8
    )(own_keep, own_came, squares, squares_came)
    own_came = cross_swap(own_send, 2, 4)

    far_send, far_keep = local_call(
        second_kernel, "second_far", [blocks(tiles, bf16), blocks(tiles, f32)], [VMEM] * 2, 8
    )(far_keep, far_came)
    far_came = cross_swap(far_send, 4, 2)
    own_send, own_keep, squares = local_call(
        second_kernel, "second_own", [blocks(tiles + 1, bf16), blocks(tiles, f32), row_sum], [VMEM] * 3, 8
    )(own_keep, own_came, squares)
    own_came = cross_swap(own_send, 4, 2)

    (far_send,) = local_call(
        third_kernel, "third_far", [blocks(tiles + 1, bf16)], [VMEM] * 3, 8
    )(far_keep, far_came, squares)
    far_came = swap(far_send, 8)
    squares_came = cross_swap(squares, 12, 10)

    states = [(local_params.shape, f32), (global_params.shape, f32), (momentum.shape, f32)]
    own_keep, squares, *parts = local_call(
        prepare_kernel,
        "prepare_ends",
        [blocks(tiles, f32), row_sum] + states + states,
        [VMEM] * 3 + [SMEM] + [VMEM] * 5,
        8,
    )(own_keep, own_came, squares, fragment_order, delta, other, local_params, global_params, momentum)

    count = FRAG * width * lax.axis_size("fsdp")
    return local_call(
        functools.partial(last_kernel, count),
        "both_ends",
        [((1, chunk, heads), f32), ((1, chunk), f32)] + states,
        [VMEM] * 12,
        8,
        [pltpu.VMEM((1, chunk, heads), f32), pltpu.VMEM((1, chunk), f32)]
        + [pltpu.VMEM(shape, dtype) for shape, dtype in states]
        + [pltpu.SemaphoreType.DMA((5,))],
        HBM,
    )(own_keep, far_came, squares, squares_came, key_weight, spread, *parts)


def scatter_sum(partial):
    count = lax.axis_size("fsdp")
    factors = fsdp_factors(count)
    place = lax.axis_index("fsdp")
    rest = partial.reshape(tuple(reversed(factors)) + (partial.shape[0] // count, partial.shape[1]))
    stride = 1
    for factor in factors:
        axis = rest.ndim - 3
        own = (place // stride) % factor
        arrived = []
        for offset in range(1, factor):
            block = lax.dynamic_index_in_dim(rest, own ^ offset, axis, keepdims=False)
            arrived.append(swap(block.astype(jnp.bfloat16), offset * stride))
        total = lax.dynamic_index_in_dim(rest, own, axis, keepdims=False)
        for block in arrived:
            total = total + block.astype(jnp.float32)
        rest = total
        stride *= factor
    return rest


def scalar_sum(value):
    count = lax.axis_size("fsdp")
    mask = 1
    while mask < count:
        value = value + swap(value, mask)
        mask *= 2
    return value


def outer_step(averaged, glob_rows, moment_rows, squares, count):
    limit = CLIP_RATE * jnp.sqrt(jnp.float32(count))
    factor = jnp.minimum(1.0, limit / jnp.sqrt(squares + EPSILON))
    clipped = averaged * factor
    moment_new = MOMENT * moment_rows + clipped
    global_new = glob_rows - OUTER_RATE * (clipped + MOMENT * moment_new)
    return (moment_new, global_new)


def inner_part(tokens, cotangent, keep_mask, key_weight, norm_gain):
    as_float = tokens.astype(jnp.float32)
    inv_rms = lax.rsqrt(jnp.mean(as_float * as_float, axis=1, keepdims=True) + EPSILON)
    unit_rows = as_float * inv_rms
    normed = unit_rows.astype(jnp.bfloat16)
    masked = jnp.where(keep_mask[:, None] == 1, cotangent, jnp.zeros_like(cotangent))
    partial_grad = jnp.einsum("td,th->dh", normed, masked, preferred_element_type=jnp.float32)
    own_grad = scatter_sum(partial_grad)
    gain_grad = jnp.sum(own_grad * key_weight[0].astype(jnp.float32), axis=1)
    weight_grad = (norm_gain[0][:, None] * own_grad)[None]
    return (weight_grad, gain_grad[None])


def outer_part(local_params, global_params, momentum, fragment_order):
    frag_rows = fragment_order[:FRAG]
    own_local = local_params[0]
    local_rows = jnp.take(own_local, frag_rows, axis=0)
    glob_rows = jnp.take(global_params, frag_rows, axis=0)
    moment_rows = jnp.take(momentum, frag_rows, axis=0)
    delta = glob_rows - local_rows
    replicas = lax.axis_size("replica")
    count = FRAG * global_params.shape[1] * lax.axis_size("fsdp")
    gathered = lax.all_gather(delta.astype(jnp.bfloat16), "replica", axis=0)
    averaged = jnp.sum(gathered.astype(jnp.float32), axis=0) / replicas
    squares = scalar_sum(jnp.sum(averaged * averaged))
    moment_new, global_new = outer_step(averaged, glob_rows, moment_rows, squares, count)
    merged = MIX_RATE * local_rows + (1.0 - MIX_RATE) * global_new
    local_out = own_local.at[frag_rows].set(merged)[None]
    global_out = global_params.at[frag_rows].set(global_new)
    moment_out = momentum.at[frag_rows].set(moment_new)
    return (local_out, global_out, moment_out)


def per_device(
    tokens,
    cotangent,
    keep_mask,
    key_weight,
    norm_gain,
    local_params,
    global_params,
    momentum,
    fragment_order,
):
    chunk = key_weight.shape[1]
    three_stages = fsdp_factors(lax.axis_size("fsdp")) == [2, 2, 4]
    aligned = chunk % PACKED_ROWS == 0 and (2 * chunk) % LANES == 0
    if three_stages and aligned and lax.axis_size("replica") == 2:
        return three_stage(
            tokens,
            cotangent,
            keep_mask,
            key_weight,
            norm_gain,
            local_params,
            global_params,
            momentum,
            fragment_order,
        )
    weight_grad, gain_grad = inner_part(tokens, cotangent, keep_mask, key_weight, norm_gain)
    local_out, global_out, moment_out = outer_part(
        local_params, global_params, momentum, fragment_order
    )
    return (weight_grad, gain_grad, local_out, global_out, moment_out)


def solution(mesh):
    in_specs = (
        P(("replica", "fsdp"), None),
        P(("replica", "fsdp"), None),
        P(("replica", "fsdp")),
        P("replica", "fsdp", None),
        P("replica", "fsdp"),
        P("replica", None, "fsdp"),
        P(None, "fsdp"),
        P(None, "fsdp"),
        P(),
    )
    out_specs = (
        P("replica", "fsdp", None),
        P("replica", "fsdp"),
        P("replica", None, "fsdp"),
        P(None, "fsdp"),
        P(None, "fsdp"),
    )
    return jax.shard_map(
        per_device, mesh=mesh, in_specs=in_specs, out_specs=out_specs, check_vma=False
    )
```
